32 devices in a mesh: groups: 2 (over y), seq: 16 (over z, x, core).
Axes of the slice: x: 2, y: 2, z: 4, core: 2. Of those that a mesh axis runs over, the one named last changes fastest.
Arguments:
- conv_input: bfloat16 [32768, 2304], P(('groups', 'seq')), parts along dimension 0, may hold values from -6 to 6
- gate_input: bfloat16 [32768, 2048], P(('groups', 'seq')), parts along dimension 0, may hold values from -6 to 6
- step_raw: bfloat16 [32768, 32], P(('groups', 'seq')), parts along dimension 0, may hold values from -1.5 to 1.5
- filter_taps: float32 [2, 4, 2304], replicated, may hold values from -3 to 3
- filter_bias: float32 [2, 2304], replicated, may hold values from -0.9 to -0.1
- step_bias: float32 [2, 32], replicated, may hold values from -4.5 to -3.5
- log_rate: float32 [2, 32], replicated
- skip_scale: float32 [2, 32], replicated, may hold values from 0.5 to 1.5
- norm_gain: float32 [2, 2048], replicated, may hold values from 0.5 to 1.5
Outputs:
- block_output: bfloat16 [32768, 2048], P(('groups', 'seq')), parts along dimension 0
The draws below stay inside these ranges and needn't reach their ends.
There are 2 independent parts, one for each index of `groups`. The reference program is written for one: setup_inputs(seed, part) draws one part's arguments, and reference() takes and returns one part's arrays. A program takes and returns all parts, laid end to end along the dimension named above; an argument that names none is the same for every part. Nothing has to cross between parts.
All inputs are finite; a program needn't handle non-finite values.
Results may differ from the reference program's by a relative error of at most 0.018.
Values may be sent and summed in bfloat16 or wider, within the bound.
A program may use at most 192 MiB of HBM per device.

```python
import math
import jax
import jax.numpy as jnp
from jax import lax

HEADS = 32
HEAD_DIM = 64
STATE = 128
CONV = 4
SPAN = 256
TOK_DEV = 1024
INNER = 2048
CHANNELS = 2304
SEQ_TOKENS = 16384


def draw_conv_input(key, part):
    value_key = jax.random.fold_in(key, 301)
    values = jax.random.normal(value_key, (SEQ_TOKENS, CHANNELS), jnp.float32)
    return jnp.clip(values, -6.0, 6.0).astype(jnp.bfloat16)


def draw_step_raw(key, part):
    level_key = jax.random.fold_in(key, 101)
    noise_key = jax.random.fold_in(key, 102)
    blocks = SEQ_TOKENS // TOK_DEV
    levels = jax.random.uniform(level_key, (blocks, HEADS), jnp.float32, math.log(0.5), math.log(2.0))
    spread = jnp.repeat(levels, TOK_DEV, axis=0)
    noise = jax.random.uniform(noise_key, (SEQ_TOKENS, HEADS), jnp.float32, -0.8, 0.8)
    return (spread + noise).astype(jnp.bfloat16)


def draw_log_rate(key, part):
    base_key = jax.random.fold_in(key, 201)
    slow_key = jax.random.fold_in(base_key, 1)
    fast_key = jax.random.fold_in(base_key, 2)
    nominal_step = 0.024
    reach = jnp.exp(jax.random.uniform(slow_key, (2, HEADS), jnp.float32, math.log(2.0), math.log(8.0)))
    slow = 1.0 / (reach * TOK_DEV * nominal_step)
    memory = jax.random.uniform(fast_key, (2, HEADS), jnp.float32, 30.0, 50.0)
    fast = 1.0 / (memory * nominal_step)
    fast_count = HEADS // 2
    ranking = jnp.stack([jax.random.permutation(jax.random.fold_in(base_key, 5 + number), HEADS) for number in range(2)])
    return jnp.log(jnp.where(ranking < fast_count, fast, slow)).astype(jnp.float32)


def steps_of(own_key, extent, cuts, least, high):
    def one(position, blocks):
        steps = jax.random.uniform(jax.random.fold_in(jax.random.fold_in(own_key, 6), position), (blocks,), jnp.float32, least / len(cuts), high / len(cuts))
        return jnp.repeat(jnp.exp(steps), extent[position] // blocks).reshape((-1,) + (1,) * (len(extent) - position - 1))

    factor_of = one(*cuts[0])
    for cut in cuts[1:]:
        factor_of = factor_of * one(*cut)
    return factor_of


def scatter_about(rng, dims, width, most, shards=(), dtype=jnp.bfloat16):
    values = jax.random.normal(rng, dims, jnp.float32) * width
    if len(shards) > 0:
        values = steps_of(rng, dims, shards, -0.22, 0.18) * values
    return jnp.clip(values, min=-most, max=most).astype(dtype)


def setup_inputs(seed: int = 0, part: int = 0) -> dict:
    arg_keys = jax.random.split(jax.random.key(seed), 10)
    part_keys = jax.random.split(jax.random.fold_in(arg_keys[9], part), 10)
    return {
        "conv_input": draw_conv_input(jax.random.fold_in(jax.random.fold_in(arg_keys[9], part), 71), part),
        "gate_input": scatter_about(part_keys[1], (SEQ_TOKENS, INNER), 1.0, 6.0, ((0, 16),)),
        "step_raw": draw_step_raw(jax.random.fold_in(jax.random.fold_in(arg_keys[9], part), 71), part),
        "filter_taps": scatter_about(arg_keys[3], (2, CONV, CHANNELS), CONV ** -0.5, 3.0, (), jnp.float32),
        "filter_bias": jnp.clip(jax.random.uniform(arg_keys[4], (2, CHANNELS), jnp.float32, -0.9, -0.1), -0.9, -0.1),
        "step_bias": jnp.clip(jax.random.uniform(arg_keys[5], (2, HEADS), jnp.float32, -4.5, -3.5), -4.5, -3.5),
        "log_rate": draw_log_rate(jax.random.fold_in(arg_keys[9], 71), part),
        "skip_scale": jnp.clip(jax.random.uniform(arg_keys[7], (2, HEADS), jnp.float32, 0.5, 1.5), 0.5, 1.5),
        "norm_gain": jnp.clip(1.0 + 0.1 * jax.random.normal(arg_keys[8], (2, INNER), jnp.float32), 0.5, 1.5),
    }


def rounded(array):
    return lax.optimization_barrier(array.astype(jnp.bfloat16)).astype(jnp.float32)

def span_math(activated, raw_rates, step_bias, decay_rate, skip_row, carried_state):
    inner_width = HEADS * HEAD_DIM
    values = activated[:, :inner_width].reshape(SPAN, HEADS, HEAD_DIM).astype(jnp.float32)
    input_map = activated[:, inner_width:inner_width + STATE]
    output_map = activated[:, inner_width + STATE:]
    step_size = jax.nn.softplus(raw_rates.astype(jnp.float32) + step_bias[None, :])
    log_decay = jnp.cumsum(step_size * decay_rate[None, :], axis=0)
    log_rows = log_decay.T
    decay_gap = log_rows[:, :, None] - log_rows[:, None, :]
    causal = jnp.arange(SPAN)[:, None] >= jnp.arange(SPAN)[None, :]
    scores = jnp.dot(output_map, input_map.T, preferred_element_type=jnp.float32)
    weights = rounded(scores[None] * jnp.exp(jnp.where(causal[None], decay_gap, -jnp.inf)) * step_size.T[:, None, :])
    local_out = jnp.einsum('hts,shp->thp', weights, values)
    scaled = rounded(values * (jnp.exp(log_decay[-1][None, :] - log_decay) * step_size)[:, :, None])
    span_state = jnp.einsum('shp,sn->hpn', scaled, input_map.astype(jnp.float32))
    carried_out = jnp.exp(log_decay)[:, :, None] * jnp.einsum('tn,hpn->thp', output_map.astype(jnp.float32), rounded(carried_state))
    result = local_out + carried_out + skip_row[None, :, None] * values
    next_state = jnp.exp(log_decay[-1])[:, None, None] * carried_state + span_state
    return (result.reshape(SPAN, inner_width).astype(jnp.bfloat16), next_state)

def direction_pass(conv_input, step_raw, taps, bias_row, step_bias, log_rate_row, skip_row):
    blocks = conv_input.shape[0] // SPAN
    channels = conv_input.shape[1]
    margin = CONV - 1
    decay_rate = -jnp.exp(log_rate_row)

    def advance(carried, inputs):
        tail_rows, carried_state = carried
        block_rows, raw_rates = inputs
        window = jnp.concatenate([tail_rows, block_rows], axis=0)
        summed = bias_row[None, :] + window[0:SPAN].astype(jnp.float32) * taps[0][None, :]
        for offset in range(1, CONV):
            summed = summed + window[offset:offset + SPAN].astype(jnp.float32) * taps[offset][None, :]
        activated = jax.nn.silu(summed).astype(jnp.bfloat16)
        result, next_state = span_math(activated, raw_rates, step_bias, decay_rate, skip_row, carried_state)
        return ((window[SPAN:], next_state), result)
    initial = (jnp.zeros((margin, channels), jnp.bfloat16), jnp.zeros((HEADS, HEAD_DIM, STATE), jnp.float32))
    finished, results = lax.scan(advance, initial, (conv_input.reshape(blocks, SPAN, channels), step_raw.reshape(blocks, SPAN, HEADS)))
    return results.reshape(blocks * SPAN, HEADS * HEAD_DIM)

def gated_norm(result, gating, gain_row):
    gated = result.astype(jnp.float32) * gating
    inverse_rms = lax.rsqrt(lax.optimization_barrier(jnp.mean(gated * gated, axis=-1, keepdims=True)) + 1e-05)
    return gated * inverse_rms * gain_row[None, :]

def reference(conv_input, gate_input, step_raw, filter_taps, filter_bias, step_bias, log_rate, skip_scale, norm_gain):
    forward = direction_pass(conv_input, step_raw, filter_taps[0], filter_bias[0], step_bias[0], log_rate[0], skip_scale[0])
    backward = jnp.flip(direction_pass(jnp.flip(conv_input, 0), jnp.flip(step_raw, 0), filter_taps[1], filter_bias[1], step_bias[1], log_rate[1], skip_scale[1]), 0)
    gating = jax.nn.silu(gate_input.astype(jnp.float32))
    combined = gated_norm(forward, gating, norm_gain[0]) + gated_norm(backward, gating, norm_gain[1])
    return combined.astype(jnp.bfloat16)
```

```python
import functools

import jax
import jax.numpy as jnp
from jax import lax
from jax.experimental import pallas as pl
from jax.experimental.pallas import tpu as pltpu
from jax.sharding import PartitionSpec as P

HEAD_DIM = 64
STATE = 128
CHUNK = 128
HALO = 16
LOG2E = 1.4426950408889634
F32 = jnp.float32
BF16 = jnp.bfloat16


def expander(heads, copies):
    row = lax.broadcasted_iota(jnp.int32, (heads * copies, heads * HEAD_DIM), 0) % heads
    col = lax.broadcasted_iota(jnp.int32, (heads * copies, heads * HEAD_DIM), 1) // HEAD_DIM
    return (row == col).astype(BF16)


def expand(values, matrix):
    high = values.astype(BF16)
    rest = values - high.astype(F32)
    low = rest.astype(BF16)
    parts = [high, low]
    heads = values.shape[1]
    if matrix.shape[0] == 3 * heads:
        parts.append((rest - low.astype(F32)).astype(BF16))
    return jnp.dot(jnp.concatenate(parts, axis=1), matrix, preferred_element_type=F32)


def prepare_kernel(
    heads,
    low_ref,
    high_ref,
    prev_ref,
    cur_ref,
    next_ref,
    raw_ref,
    taps_ref,
    bias_ref,
    sbias_ref,
    lrate_ref,
    e2_ref,
    e3_ref,
    u_ref,
    piece_ref,
    col_ref,
    row_ref,
    last_ref,
    dec_ref,
    buf,
    state,
    run,
):
    i = pl.program_id(0)
    count = pl.num_programs(0)
    inner = heads * HEAD_DIM
    channels = cur_ref.shape[1]

    @pl.when(i == 0)
    def _():
        buf[0:HALO] = low_ref[...].astype(F32)
        state[...] = jnp.zeros_like(state)
        run[...] = jnp.zeros_like(run)

    @pl.when(i > 0)
    def _():
        buf[0:HALO] = prev_ref[...].astype(F32)

    buf[HALO : HALO + CHUNK] = cur_ref[...].astype(F32)

    @pl.when(i == count - 1)
    def _():
        buf[HALO + CHUNK :] = high_ref[...].astype(F32)

    @pl.when(i < count - 1)
    def _():
        buf[HALO + CHUNK :] = next_ref[...].astype(F32)

    width = 256
    for c in range(channels // width):
        lanes = slice(c * width, (c + 1) * width)
        for k in range(2):
            half = None
            for j in range(4):
                start = HALO + (j - 3 if k == 0 else 3 - j)
                term = buf[start : start + CHUNK, lanes] * (0.5 * taps_ref[k, j : j + 1, lanes])
                half = 0.5 * bias_ref[k : k + 1, lanes] + term if half is None else half + term
            u_ref[k, :, lanes] = (half + half * jnp.tanh(half)).astype(BF16)

    t = lax.broadcasted_iota(jnp.int32, (CHUNK, CHUNK), 0)
    s = lax.broadcasted_iota(jnp.int32, (CHUNK, CHUNK), 1)
    raw = raw_ref[...].astype(F32)
    for k in range(2):
        dt = jax.nn.softplus(raw + sbias_ref[k : k + 1, :])
        a = dt * (-LOG2E * jnp.exp(lrate_ref[k : k + 1, :]))
        tri = ((s <= t) if k == 0 else (s >= t)).astype(F32)
        cum = jnp.dot(tri, a, precision=lax.Precision.HIGHEST, preferred_element_type=F32)
        end = cum[CHUNK - 1 : CHUNK] if k == 0 else cum[0:1]
        ahead = jnp.log2(dt) - cum
        col_ref[:, k * heads : (k + 1) * heads] = cum
        row_ref[k * heads : (k + 1) * heads, :] = ahead.T
        weight = expand(jnp.exp2(end + ahead), e2_ref[...])
        xs = (u_ref[k, :, :inner].astype(F32) * weight).astype(BF16)
        bt = u_ref[k, :, inner : inner + STATE].T
        piece = jnp.dot(bt, xs, preferred_element_type=F32)
        piece_ref[k, 0] = piece.astype(BF16)
        before = run[k : k + 1, :]
        if k == 0:
            factor = expand(jnp.broadcast_to(jnp.exp2(end), (8, heads)), e3_ref[...])[0:1]
            state[0] = state[0] * factor + piece
        else:
            factor = expand(jnp.broadcast_to(jnp.exp2(before), (8, heads)), e3_ref[...])[0:1]
            state[1] = state[1] + piece * factor
        run[k : k + 1, :] = before + end

    @pl.when(i == count - 1)
    def _():
        last_ref[...] = state[...].astype(BF16)
        dec_ref[...] = run[...]


def diagonal_kernel(heads, u_ref, col_ref, row_ref, skip_ref, y_ref):
    inner = heads * HEAD_DIM
    t = lax.broadcasted_iota(jnp.int32, (CHUNK, CHUNK), 0)
    s = lax.broadcasted_iota(jnp.int32, (CHUNK, CHUNK), 1)
    lane = lax.broadcasted_iota(jnp.int32, (CHUNK, CHUNK), 1)
    for k in range(2):
        b = u_ref[k, :, inner : inner + STATE]
        c = u_ref[k, :, inner + STATE :]
        scores = lax.dot_general(c, b, (((1,), (1,)), ((), ())), preferred_element_type=F32)
        scores = jnp.where((s <= t) if k == 0 else (s >= t), scores, 0.0)
        for pair in range(heads // 2):
            lanes = slice(pair * 128, (pair + 1) * 128)
            x = u_ref[k, :, lanes]
            weights = []
            for h in (2 * pair, 2 * pair + 1):
                n = k * heads + h
                gap = col_ref[:, n : n + 1] + row_ref[n : n + 1, :]
                weights.append((scores * jnp.exp2(jnp.minimum(gap, 64.0))).astype(BF16))
            zero = jnp.zeros_like(x)
            both = jnp.concatenate(
                [jnp.where(lane < HEAD_DIM, x, zero), jnp.where(lane >= HEAD_DIM, x, zero)], axis=0
            )
            y = jnp.dot(jnp.concatenate(weights, axis=1), both, preferred_element_type=F32)
            y_ref[k, :, lanes] = (y + x.astype(F32) * skip_ref[k : k + 1, lanes]).astype(BF16)


def finish_kernel(
    heads,
    y_ref,
    c_ref,
    col_ref,
    piece_ref,
    in_ref,
    gate_ref,
    gain_ref,
    e2_ref,
    e3_ref,
    out_ref,
    state,
    kept,
):
    step = pl.program_id(0)
    i = pl.program_id(1)
    count = pl.num_programs(1)

    @pl.when(i == 0)
    def _():
        state[...] = in_ref[0].astype(F32)

    def part(k):
        cum = col_ref[:, k * heads : (k + 1) * heads]
        end = cum[CHUNK - 1 : CHUNK] if k == 0 else cum[0:1]
        scale = expand(jnp.exp2(cum), e2_ref[...])
        carried = jnp.dot(c_ref[0], state[...].astype(BF16), preferred_element_type=F32)
        y = y_ref[0].astype(F32) + scale * carried
        half = 0.5 * gate_ref[...].astype(F32)
        g = y * (half + half * jnp.tanh(half))
        inverse = lax.rsqrt(jnp.mean(g * g, axis=-1, keepdims=True) + 1e-05)
        factor = expand(jnp.broadcast_to(jnp.exp2(end), (8, heads)), e3_ref[...])[0:1]
        state[...] = state[...] * factor + piece_ref[0, 0].astype(F32)
        return g * inverse * gain_ref[k : k + 1, :]

    @pl.when(step == 0)
    def _():
        at = pl.multiple_of((count - 1 - i) * CHUNK, CHUNK)
        kept[pl.ds(at, CHUNK), :] = part(1)

    @pl.when(step == 1)
    def _():
        at = pl.multiple_of(i * CHUNK, CHUNK)
        out_ref[...] = (kept[pl.ds(at, CHUNK), :] + part(0)).astype(BF16)


def passed_along(shard, by):
    devices = lax.axis_size("seq")
    pairs = [(i, i + by) for i in range(devices) if 0 <= i + by < devices]
    return lax.ppermute(shard, "seq", pairs)


def on_device(
    conv_input,
    gate_input,
    step_raw,
    filter_taps,
    filter_bias,
    step_bias,
    log_rate,
    skip_scale,
    norm_gain,
):
    length, channels = conv_input.shape
    heads = step_raw.shape[1]
    inner = heads * HEAD_DIM
    chunks = length // CHUNK
    low = passed_along(conv_input[length - HALO :], 1)
    high = passed_along(conv_input[:HALO], -1)
    e2 = expander(heads, 2)
    e3 = expander(heads, 3)
    per = CHUNK // HALO
    whole = lambda *shape: pl.BlockSpec(shape, lambda *_: (0,) * len(shape))
    params = pltpu.CompilerParams(vmem_limit_bytes=48 * 1024 * 1024)

    u, piece, col, row, last, dec = pl.pallas_call(
        functools.partial(prepare_kernel, heads),
        grid=(chunks,),
        in_specs=[
            whole(HALO, channels),
            whole(HALO, channels),
            pl.BlockSpec((HALO, channels), lambda i: (jnp.maximum(i * per - 1, 0), 0)),
            pl.BlockSpec((CHUNK, channels), lambda i: (i, 0)),
            pl.BlockSpec(
                (HALO, channels), lambda i: (jnp.minimum(i * per + per, chunks * per - 1), 0)
            ),
            pl.BlockSpec((CHUNK, heads), lambda i: (i, 0)),
            whole(*filter_taps.shape),
            whole(*filter_bias.shape),
            whole(2, heads),
            whole(2, heads),
            whole(*e2.shape),
            whole(*e3.shape),
        ],
        out_specs=[
            pl.BlockSpec((2, CHUNK, channels), lambda i: (0, i, 0)),
            pl.BlockSpec((2, 1, STATE, inner), lambda i: (0, i, 0, 0)),
            pl.BlockSpec((CHUNK, 2 * heads), lambda i: (i, 0)),
            pl.BlockSpec((2 * heads, CHUNK), lambda i: (0, i)),
            whole(2, STATE, inner),
            whole(2, heads),
        ],
        out_shape=[
            jax.ShapeDtypeStruct((2, length, channels), BF16),
            jax.ShapeDtypeStruct((2, chunks, STATE, inner), BF16),
            jax.ShapeDtypeStruct((length, 2 * heads), F32),
            jax.ShapeDtypeStruct((2 * heads, length), F32),
            jax.ShapeDtypeStruct((2, STATE, inner), BF16),
            jax.ShapeDtypeStruct((2, heads), F32),
        ],
        scratch_shapes=[
            pltpu.VMEM((CHUNK + 2 * HALO, channels), F32),
            pltpu.VMEM((2, STATE, inner), F32),
            pltpu.VMEM((2, heads), F32),
        ],
        compiler_params=params,
        cost_estimate=pl.CostEstimate(
            flops=2 * 2 * length * STATE * inner, bytes_accessed=25_000_000, transcendentals=0
        ),
    )(
        low,
        high,
        conv_input,
        conv_input,
        conv_input,
        step_raw,
        filter_taps,
        filter_bias,
        step_bias,
        log_rate,
        e2,
        e3,
    )

    def wide(logs):
        return jnp.repeat(jnp.exp2(logs), HEAD_DIM)[None, :]

    devices = lax.axis_size("seq")
    arriving = []
    for k in range(2):
        sign = 1 if k == 0 else -1
        total, held = passed_along((dec[k], last[k]), sign)
        held = held.astype(F32)
        offset = 1
        while offset < devices - 1:
            other, came = passed_along((total, held.astype(BF16)), sign * offset)
            held = held + wide(total) * came.astype(F32)
            total = total + other
            offset *= 2
        arriving.append(held.astype(BF16))

    local = pl.pallas_call(
        functools.partial(diagonal_kernel, heads),
        grid=(chunks,),
        in_specs=[
            pl.BlockSpec((2, CHUNK, channels), lambda i: (0, i, 0)),
            pl.BlockSpec((CHUNK, 2 * heads), lambda i: (i, 0)),
            pl.BlockSpec((2 * heads, CHUNK), lambda i: (0, i)),
            whole(2, inner),
        ],
        out_specs=pl.BlockSpec((2, CHUNK, inner), lambda i: (0, i, 0)),
        out_shape=jax.ShapeDtypeStruct((2, length, inner), BF16),
        compiler_params=params,
        cost_estimate=pl.CostEstimate(
            flops=20 * 2 * length * CHUNK * inner, bytes_accessed=20_000_000, transcendentals=0
        ),
    )(u, col, row, jnp.repeat(skip_scale, HEAD_DIM, axis=1))

    entering = jnp.stack(arriving)
    at = lambda p, i: jnp.where(p == 0, chunks - 1 - i, i)
    return pl.pallas_call(
        functools.partial(finish_kernel, heads),
        grid=(2, chunks),
        in_specs=[
            pl.BlockSpec((1, CHUNK, inner), lambda p, i: (1 - p, at(p, i), 0)),
            pl.BlockSpec((1, CHUNK, STATE), lambda p, i: (1 - p, at(p, i), inner // STATE + 1)),
            pl.BlockSpec((CHUNK, 2 * heads), lambda p, i: (at(p, i), 0)),
            pl.BlockSpec((1, 1, STATE, inner), lambda p, i: (1 - p, at(p, i), 0, 0)),
            pl.BlockSpec((1, STATE, inner), lambda p, i: (1 - p, 0, 0)),
            pl.BlockSpec((CHUNK, inner), lambda p, i: (at(p, i), 0)),
            whole(2, inner),
            whole(*e2.shape),
            whole(*e3.shape),
        ],
        out_specs=pl.BlockSpec((CHUNK, inner), lambda p, i: (jnp.where(p == 0, 0, i), 0)),
        out_shape=jax.ShapeDtypeStruct((length, inner), BF16),
        scratch_shapes=[
            pltpu.VMEM((STATE, inner), F32),
            pltpu.VMEM((length, inner), F32),
        ],
        compiler_params=params,
        cost_estimate=pl.CostEstimate(
            flops=2 * 2 * length * STATE * inner, bytes_accessed=30_000_000, transcendentals=0
        ),
    )(local, u, col, piece, entering, gate_input, norm_gain, e2, e3)


def solution(mesh):
    return jax.shard_map(
        on_device,
        mesh=mesh,
        in_specs=(P(("groups", "seq"), None),) * 3 + (P(),) * 6,
        out_specs=P(("groups", "seq"), None),
        check_vma=False,
    )
```

```python
import functools

import jax
import jax.numpy as jnp
from jax import lax
from jax.experimental import pallas as pl
from jax.experimental.pallas import tpu as pltpu
from jax.sharding import PartitionSpec as P

HEAD_DIM = 64
STATE = 128
CHUNK = 128
HALO = 16
TILE = 16
MESH = pl.DeviceIdType.MESH
LOG2E = 1.4426950408889634
F32 = jnp.float32
BF16 = jnp.bfloat16


def expander(heads, copies):
    row = lax.broadcasted_iota(jnp.int32, (heads * copies, heads * HEAD_DIM), 0) % heads
    col = lax.broadcasted_iota(jnp.int32, (heads * copies, heads * HEAD_DIM), 1) // HEAD_DIM
    return (row == col).astype(BF16)


def expand(values, matrix):
    high = values.astype(BF16)
    rest = values - high.astype(F32)
    low = rest.astype(BF16)
    parts = [high, low]
    heads = values.shape[1]
    if matrix.shape[0] == 3 * heads:
        parts.append((rest - low.astype(F32)).astype(BF16))
    return jnp.dot(jnp.concatenate(parts, axis=1), matrix, preferred_element_type=F32)


def mixer_kernel(
    heads,
    n,
    tail_ref,
    head_ref,
    prev_ref,
    cur_ref,
    next_ref,
    raw_ref,
    gate_ref,
    taps_ref,
    bias_ref,
    sbias_ref,
    lrate_ref,
    skip_ref,
    gain_ref,
    e2_ref,
    e3_ref,
    out_ref,
    buf,
    u,
    piece,
    local,
    kept,
    cols,
    rows,
    state,
    run,
    edge,
    halo,
    message,
    got,
    reply,
    entering,
    edge_send,
    edge_recv,
    send_sem,
    recv_sem,
):
    step = pl.program_id(0)
    chunks = u.shape[1]
    inner = heads * HEAD_DIM
    channels = cur_ref.shape[1]
    me = lax.axis_index("seq")
    height = STATE * (inner // 128) // n
    share = lambda o: (
        slice(o * height % STATE, o * height % STATE + height),
        slice(o * height // STATE * 128, o * height // STATE * 128 + 128),
    )

    def to_edge(side):
        return pltpu.make_async_remote_copy(
            src_ref=edge.at[side],
            dst_ref=halo.at[side],
            send_sem=edge_send.at[side],
            recv_sem=edge_recv.at[side],
            device_id={"seq": lax.rem(me + (1 if side == 0 else n - 1), n)},
            device_id_type=MESH,
        )

    def to_all(source, target, number, k):
        @pl.loop(1, n)
        def _(p):
            peer = lax.rem(me + p, n)
            pltpu.make_async_remote_copy(
                src_ref=source.at[k, peer],
                dst_ref=target.at[k, me],
                send_sem=send_sem.at[number],
                recv_sem=recv_sem.at[number],
                device_id={"seq": peer},
                device_id_type=MESH,
            ).start()

    def wait_all(ref, sem, k):
        part = ref.at[k, pl.ds(0, n - 1)]
        pltpu.make_async_copy(part, part, sem).wait()

    @pl.when(step == 0)
    def _():
        barrier = pltpu.get_barrier_semaphore()

        @pl.loop(1, n)
        def _(p):
            pl.semaphore_signal(
                barrier, inc=1, device_id={"seq": lax.rem(me + p, n)}, device_id_type=MESH
            )

        edge[0] = tail_ref[...]
        edge[1] = head_ref[...]
        pl.semaphore_wait(barrier, n - 1)
        to_edge(0).start()
        to_edge(1).start()

    t = lax.broadcasted_iota(jnp.int32, (CHUNK, CHUNK), 0)
    s = lax.broadcasted_iota(jnp.int32, (CHUNK, CHUNK), 1)

    def prepare(k, at, first, last):
        @pl.when(first)
        def _():
            state[...] = jnp.zeros_like(state)
            run[...] = jnp.zeros_like(run)

        buf[0:HALO] = prev_ref[...].astype(F32)
        buf[HALO : HALO + CHUNK] = cur_ref[...].astype(F32)
        buf[HALO + CHUNK :] = next_ref[...].astype(F32)

        @pl.when(last)
        def _():
            to_edge(k).wait()
            if k == 0:
                buf[0:HALO] = jnp.where(me == 0, 0.0, halo[0].astype(F32))
            else:
                buf[HALO + CHUNK :] = jnp.where(me == n - 1, 0.0, halo[1].astype(F32))

        width = 256
        for c in range(channels // width):
            lanes = slice(c * width, (c + 1) * width)
            half = None
            for j in range(4):
                start = HALO + (j - 3 if k == 0 else 3 - j)
                term = buf[start : start + CHUNK, lanes] * (0.5 * taps_ref[k, j : j + 1, lanes])
                half = 0.5 * bias_ref[k : k + 1, lanes] + term if half is None else half + term
            u[k, at, :, lanes] = (half + half * jnp.tanh(half)).astype(BF16)

        dt = jax.nn.softplus(raw_ref[...].astype(F32) + sbias_ref[k : k + 1, :])
        a = dt * (-LOG2E * jnp.exp(lrate_ref[k : k + 1, :]))
        tri = ((s <= t) if k == 0 else (s >= t)).astype(F32)
        cum = jnp.dot(tri, a, precision=lax.Precision.HIGHEST, preferred_element_type=F32)
        end = cum[CHUNK - 1 : CHUNK] if k == 0 else cum[0:1]
        ahead = jnp.log2(dt) - cum
        cols[k, at] = cum
        rows[k, at] = ahead.T
        weight = expand(jnp.exp2(end + ahead), e2_ref[...])
        xs = (u[k, at, :, :inner].astype(F32) * weight).astype(BF16)
        bt = u[k, at, :, inner : inner + STATE].T
        part = jnp.dot(bt, xs, preferred_element_type=F32)
        piece[k, at] = part.astype(BF16)
        before = run[0:1, :]
        factor = expand(jnp.broadcast_to(jnp.exp2(before), (8, heads)), e3_ref[...])[0:1]
        state[...] = state[...] + part * factor
        run[0:1, :] = before + end

        @pl.when(last)
        def _():
            decay = expand(jnp.exp2(jnp.broadcast_to(run[0:1, :], (TILE, heads))), e3_ref[...])
            high = decay.astype(BF16).astype(F32)
            which = lax.broadcasted_iota(jnp.int32, (TILE, inner), 0)
            tile = jnp.where(which == 0, high, jnp.where(which == 1, decay - high, 0.0))
            for o in range(n):
                where = share(o)
                message[k, o, 0:height] = state[where].astype(BF16)
                message[k, o, height:] = tile[:, where[1]].astype(BF16)
            got[k, me] = message[k, me]
            to_all(message, got, k, k)

    def scan(k):
        wait_all(got, recv_sem.at[k], k)

        def one(j, held):
            j = j if k == 0 else n - 1 - j
            reply[k, j] = held.astype(BF16)
            tile = got[k, j, height:].astype(F32)
            return held * (tile[0:1] + tile[1:2]) + got[k, j, 0:height].astype(F32)

        lax.fori_loop(0, n, one, jnp.zeros((height, 128), F32))
        entering[k, me] = reply[k, me]
        to_all(reply, entering, 2 + k, k)

    def diagonal(k, at):
        b = u[k, at, :, inner : inner + STATE]
        c = u[k, at, :, inner + STATE :]
        scores = lax.dot_general(c, b, (((1,), (1,)), ((), ())), preferred_element_type=F32)
        scores = jnp.where((s <= t) if k == 0 else (s >= t), scores, 0.0)
        for pair in range(heads // 2):
            lanes = slice(pair * 128, (pair + 1) * 128)
            x = u[k, at, :, lanes]
            weights = []
            for h in (2 * pair, 2 * pair + 1):
                gap = cols[k, at, :, h : h + 1] + rows[k, at, h : h + 1, :]
                weights.append((scores * jnp.exp2(jnp.minimum(gap, 64.0))).astype(BF16))
            zero = jnp.zeros_like(x)
            both = jnp.concatenate(
                [jnp.where(s < HEAD_DIM, x, zero), jnp.where(s >= HEAD_DIM, x, zero)], axis=0
            )
            y = jnp.dot(jnp.concatenate(weights, axis=1), both, preferred_element_type=F32)
            local[k, at, :, lanes] = (y + x.astype(F32) * skip_ref[k : k + 1, lanes]).astype(BF16)

    def finish(k, at, first):
        @pl.when(first)
        def _():
            wait_all(entering, recv_sem.at[2 + k], k)
            for o in range(n):
                state[share(o)] = entering[k, o].astype(F32)

        cum = cols[k, at]
        end = cum[CHUNK - 1 : CHUNK] if k == 0 else cum[0:1]
        scale = expand(jnp.exp2(cum), e2_ref[...])
        carried = jnp.dot(
            u[k, at, :, inner + STATE :], state[...].astype(BF16), preferred_element_type=F32
        )
        y = local[k, at].astype(F32) + scale * carried
        half = 0.5 * gate_ref[...].astype(F32)
        g = y * (half + half * jnp.tanh(half))
        inverse = lax.rsqrt(jnp.mean(g * g, axis=-1, keepdims=True) + 1e-05)
        factor = expand(jnp.broadcast_to(jnp.exp2(end), (8, heads)), e3_ref[...])[0:1]
        state[...] = state[...] * factor + piece[k, at].astype(F32)
        return g * inverse * gain_ref[k : k + 1, :]

    @pl.when(step < chunks)
    def _():
        prepare(0, chunks - 1 - step, step == 0, step == chunks - 1)

    @pl.when((step >= chunks) & (step < 2 * chunks))
    def _():
        prepare(1, step - chunks, step == chunks, step == 2 * chunks - 1)

    @pl.when(step == 2 * chunks)
    def _():
        scan(0)

    @pl.when(step == 3 * chunks - 2)
    def _():
        scan(1)

    @pl.when((step >= 2 * chunks) & (step < 3 * chunks))
    def _():
        at = step - 2 * chunks
        diagonal(0, at)
        diagonal(1, at)

    @pl.when((step >= 3 * chunks) & (step < 4 * chunks))
    def _():
        at = step - 3 * chunks
        kept[at] = finish(0, at, step == 3 * chunks)

    @pl.when(step >= 4 * chunks)
    def _():
        at = 5 * chunks - 1 - step
        out_ref[...] = (kept[at] + finish(1, at, step == 4 * chunks)).astype(BF16)

    @pl.when(step == 5 * chunks - 1)
    def _():
        for k in range(2):
            wait_all(message, send_sem.at[k], k)
            wait_all(reply, send_sem.at[2 + k], k)


def on_device(
    conv_input,
    gate_input,
    step_raw,
    filter_taps,
    filter_bias,
    step_bias,
    log_rate,
    skip_scale,
    norm_gain,
):
    length, channels = conv_input.shape
    heads = step_raw.shape[1]
    inner = heads * HEAD_DIM
    chunks = length // CHUNK
    n = lax.axis_size("seq")
    height = STATE * (inner // 128) // n
    e2 = expander(heads, 2)
    e3 = expander(heads, 3)
    per = CHUNK // HALO
    last = chunks * per - 1
    whole = lambda *shape: pl.BlockSpec(shape, lambda *_: (0,) * len(shape))

    def taken(i):
        return jnp.where(i < chunks, chunks - 1 - i, jnp.minimum(i - chunks, chunks - 1))

    def given(i):
        return jnp.where(i < 4 * chunks, jnp.clip(i - 3 * chunks, 0, chunks - 1), 5 * chunks - 1 - i)

    return pl.pallas_call(
        functools.partial(mixer_kernel, heads, n),
        grid=(5 * chunks,),
        in_specs=[
            pl.BlockSpec((HALO, channels), lambda i: (last, 0)),
            pl.BlockSpec((HALO, channels), lambda i: (0, 0)),
            pl.BlockSpec((HALO, channels), lambda i: (jnp.maximum(taken(i) * per - 1, 0), 0)),
            pl.BlockSpec((CHUNK, channels), lambda i: (taken(i), 0)),
            pl.BlockSpec((HALO, channels), lambda i: (jnp.minimum(taken(i) * per + per, last), 0)),
            pl.BlockSpec((CHUNK, heads), lambda i: (taken(i), 0)),
            pl.BlockSpec((CHUNK, inner), lambda i: (given(i), 0)),
            whole(*filter_taps.shape),
            whole(*filter_bias.shape),
            whole(2, heads),
            whole(2, heads),
            whole(2, inner),
            whole(2, inner),
            whole(*e2.shape),
            whole(*e3.shape),
        ],
        out_specs=pl.BlockSpec(
            (CHUNK, inner), lambda i: (jnp.minimum(5 * chunks - 1 - i, chunks - 1), 0)
        ),
        out_shape=jax.ShapeDtypeStruct((length, inner), BF16),
        scratch_shapes=[
            pltpu.VMEM((CHUNK + 2 * HALO, channels), F32),
            pltpu.VMEM((2, chunks, CHUNK, channels), BF16),
            pltpu.VMEM((2, chunks, STATE, inner), BF16),
            pltpu.VMEM((2, chunks, CHUNK, inner), BF16),
            pltpu.VMEM((chunks, CHUNK, inner), F32),
            pltpu.VMEM((2, chunks, CHUNK, heads), F32),
            pltpu.VMEM((2, chunks, heads, CHUNK), F32),
            pltpu.VMEM((STATE, inner), F32),
            pltpu.VMEM((8, heads), F32),
            pltpu.VMEM((2, HALO, channels), BF16),
            pltpu.VMEM((2, HALO, channels), BF16),
            pltpu.VMEM((2, n, height + TILE, 128), BF16),
            pltpu.VMEM((2, n, height + TILE, 128), BF16),
            pltpu.VMEM((2, n, height, 128), BF16),
            pltpu.VMEM((2, n, height, 128), BF16),
            pltpu.SemaphoreType.DMA((2,)),
            pltpu.SemaphoreType.DMA((2,)),
            pltpu.SemaphoreType.DMA((4,)),
            pltpu.SemaphoreType.DMA((4,)),
        ],
        compiler_params=pltpu.CompilerParams(
            collective_id=0, has_side_effects=True, vmem_limit_bytes=60 * 1024 * 1024
        ),
    )(
        conv_input,
        conv_input,
        conv_input,
        conv_input,
        conv_input,
        step_raw,
        gate_input,
        filter_taps,
        filter_bias,
        step_bias,
        log_rate,
        jnp.repeat(skip_scale, HEAD_DIM, axis=1),
        norm_gain,
        e2,
        e3,
    )


def solution(mesh):
    return jax.shard_map(
        on_device,
        mesh=mesh,
        in_specs=(P(("groups", "seq"), None),) * 3 + (P(),) * 6,
        out_specs=P(("groups", "seq"), None),
        check_vma=False,
    )
```

```python
import functools

import jax
import jax.numpy as jnp
from jax import lax
from jax.experimental import pallas as pl
from jax.experimental.pallas import tpu as pltpu
from jax.sharding import PartitionSpec as P

HEAD_DIM = 64
STATE = 128
CHUNK = 128
HALO = 16
TILE = 16
AT = ((1, 5, 9), (1, 5, 9))
MESH = pl.DeviceIdType.MESH
LOG2E = 1.4426950408889634
F32 = jnp.float32
BF16 = jnp.bfloat16


def expander(heads, copies):
    row = lax.broadcasted_iota(jnp.int32, (heads * copies, heads * HEAD_DIM), 0) % heads
    col = lax.broadcasted_iota(jnp.int32, (heads * copies, heads * HEAD_DIM), 1) // HEAD_DIM
    return (row == col).astype(BF16)


def expand(values, matrix):
    high = values.astype(BF16)
    rest = values - high.astype(F32)
    low = rest.astype(BF16)
    parts = [high, low]
    heads = values.shape[1]
    if matrix.shape[0] == 3 * heads:
        parts.append((rest - low.astype(F32)).astype(BF16))
    return jnp.dot(jnp.concatenate(parts, axis=1), matrix, preferred_element_type=F32)


def mixer_kernel(
    heads,
    n,
    tail_ref,
    head_ref,
    prev_ref,
    cur_ref,
    next_ref,
    raw_ref,
    gate_ref,
    taps_ref,
    bias_ref,
    sbias_ref,
    lrate_ref,
    skip_ref,
    gain_ref,
    out_ref,
    buf,
    u,
    piece,
    local,
    kept,
    cols,
    rows,
    state,
    run,
    edge,
    halo,
    message,
    other,
    summary,
    got,
    reply,
    entering,
    beside,
    e2_ref,
    e3_ref,
    skip,
    edge_send,
    edge_recv,
    send_sem,
    recv_sem,
):
    step = pl.program_id(0)
    chunks = u.shape[1]
    inner = heads * HEAD_DIM
    channels = cur_ref.shape[1]
    me = lax.axis_index("seq")
    chips = n // 2
    chip = me // 2
    core = lax.rem(me, 2)
    partner = me + 1 - 2 * core
    height = STATE * (inner // 128) // n
    share = lambda o: (
        slice(o * height % STATE, o * height % STATE + height),
        slice(o * height // STATE * 128, o * height // STATE * 128 + 128),
    )

    def to_edge(side):
        return pltpu.make_async_remote_copy(
            src_ref=edge.at[side],
            dst_ref=halo.at[side],
            send_sem=edge_send.at[side],
            recv_sem=edge_recv.at[side],
            device_id={"seq": lax.rem(me + (1 if side == 0 else n - 1), n)},
            device_id_type=MESH,
        )

    def to_partner(source, target, number, k):
        return pltpu.make_async_remote_copy(
            src_ref=source.at[k],
            dst_ref=target.at[k],
            send_sem=send_sem.at[number, k],
            recv_sem=recv_sem.at[number, k],
            device_id={"seq": partner},
            device_id_type=MESH,
        )

    def to_chips(source, target, number, k):
        @pl.loop(1, chips)
        def _(p):
            peer = lax.rem(chip + p, chips)
            pltpu.make_async_remote_copy(
                src_ref=source.at[k, peer],
                dst_ref=target.at[k, chip],
                send_sem=send_sem.at[number, k],
                recv_sem=recv_sem.at[number, k],
                device_id={"seq": 2 * peer + core},
                device_id_type=MESH,
            ).start()

    def wait_chips(ref, sem, number, k):
        part = ref.at[k, pl.ds(0, chips - 1)]
        pltpu.make_async_copy(part, part, sem.at[number, k]).wait()

    @pl.when(step == 0)
    def _():
        barrier = pltpu.get_barrier_semaphore()

        def greet(peer):
            pl.semaphore_signal(barrier, inc=1, device_id={"seq": peer}, device_id_type=MESH)

        greet(lax.rem(me + 1, n))
        greet(lax.rem(me + n - 1, n))

        @pl.loop(1, chips)
        def _(p):
            greet(2 * lax.rem(chip + p, chips) + core)

        edge[0] = tail_ref[...]
        edge[1] = head_ref[...]
        e2_ref[...] = expander(heads, 2)
        e3_ref[...] = expander(heads, 3)
        scales = jnp.concatenate([skip_ref[...]] * 4, axis=0)
        skip[...] = expand(scales, e3_ref[...])
        pl.semaphore_wait(barrier, chips + 1)
        to_edge(0).start()
        to_edge(1).start()

    t = lax.broadcasted_iota(jnp.int32, (CHUNK, CHUNK), 0)
    s = lax.broadcasted_iota(jnp.int32, (CHUNK, CHUNK), 1)

    def prepare(k, at, first, last):
        @pl.when(first)
        def _():
            state[...] = jnp.zeros_like(state)
            run[...] = jnp.zeros_like(run)

        buf[0:HALO] = prev_ref[...].astype(F32)
        buf[HALO : HALO + CHUNK] = cur_ref[...].astype(F32)
        buf[HALO + CHUNK :] = next_ref[...].astype(F32)

        @pl.when(last)
        def _():
            to_edge(k).wait()
            if k == 0:
                buf[0:HALO] = jnp.where(me == 0, 0.0, halo[0].astype(F32))
            else:
                buf[HALO + CHUNK :] = jnp.where(me == n - 1, 0.0, halo[1].astype(F32))

        width = 256
        for c in range(channels // width):
            lanes = slice(c * width, (c + 1) * width)
            half = None
            for j in range(4):
                start = HALO + (j - 3 if k == 0 else 3 - j)
                term = buf[start : start + CHUNK, lanes] * (0.5 * taps_ref[k, j : j + 1, lanes])
                half = 0.5 * bias_ref[k : k + 1, lanes] + term if half is None else half + term
            u[k, at, :, lanes] = (half + half * jnp.tanh(half)).astype(BF16)

        dt = jax.nn.softplus(raw_ref[...].astype(F32) + sbias_ref[:, k : k + 1])
        a = dt * (-LOG2E * jnp.exp(lrate_ref[:, k : k + 1]))
        tri = ((t <= s) if k == 0 else (t >= s)).astype(F32)
        across = jnp.dot(a, tri, precision=lax.Precision.HIGHEST, preferred_element_type=F32)
        rows[k, at] = jnp.log2(dt) - across
        cum = across.T
        ahead = rows[k, at].T
        end = cum[CHUNK - 1 : CHUNK] if k == 0 else cum[0:1]
        cols[k, at] = cum
        weight = expand(jnp.exp2(end + ahead), e2_ref[...])
        xs = (u[k, at, :, :inner].astype(F32) * weight).astype(BF16)
        bt = u[k, at, :, inner : inner + STATE].T
        part = jnp.dot(bt, xs, preferred_element_type=F32)
        piece[k, at] = part.astype(BF16)
        before = run[0:1, :]
        factor = expand(jnp.broadcast_to(jnp.exp2(before), (8, heads)), e3_ref[...])[0:1]
        state[...] = state[...] + part * factor
        run[0:1, :] = before + end

        @pl.when(last)
        def _():
            decay = expand(jnp.exp2(jnp.broadcast_to(run[0:1, :], (TILE, heads))), e3_ref[...])
            high = decay.astype(BF16).astype(F32)
            which = lax.broadcasted_iota(jnp.int32, (TILE, inner), 0)
            tile = jnp.where(which == 0, high, jnp.where(which == 1, decay - high, 0.0))
            for o in range(n):
                where = share(o)
                message[k, o, 0:height] = state[where].astype(BF16)
                message[k, o, height:] = tile[:, where[1]].astype(BF16)
            to_partner(message, other, 0, k).start()

    def decay_of(tile):
        return tile[0:1].astype(F32) + tile[1:2].astype(F32)

    def per_chip(k):
        to_partner(message, other, 0, k).wait()
        mine_first = core == k
        which = lax.broadcasted_iota(jnp.int32, (TILE, 128), 0)

        @pl.loop(0, chips)
        def _(q):
            o = 2 * q + core
            mine = message[k, o, 0:height].astype(F32)
            theirs = other[k, o, 0:height].astype(F32)
            my_decay = decay_of(message[k, o, height:])
            their_decay = decay_of(other[k, o, height:])
            total = jnp.where(mine_first, mine * their_decay + theirs, theirs * my_decay + mine)
            decay = my_decay * their_decay
            high = decay.astype(BF16).astype(F32)
            tile = jnp.where(which == 0, high, jnp.where(which == 1, decay - high, 0.0))
            summary[k, q, 0:height] = total.astype(BF16)
            summary[k, q, height:] = tile.astype(BF16)

        got[k, chip] = summary[k, chip]
        to_chips(summary, got, 1, k)

    def scan(k):
        wait_chips(got, recv_sem, 1, k)

        def one(j, held):
            j = j if k == 0 else chips - 1 - j
            reply[k, j] = held.astype(BF16)
            decay = decay_of(got[k, j, height:])
            return held * decay + got[k, j, 0:height].astype(F32)

        lax.fori_loop(0, chips, one, jnp.zeros((height, 128), F32))
        entering[k, chip] = reply[k, chip]
        to_chips(reply, entering, 2, k)

    def back(k):
        wait_chips(entering, recv_sem, 2, k)
        to_partner(entering, beside, 3, k).start()

    def diagonal(k, at):
        b = u[k, at, :, inner : inner + STATE]
        c = u[k, at, :, inner + STATE :]
        scores = lax.dot_general(c, b, (((1,), (1,)), ((), ())), preferred_element_type=F32)
        scores = jnp.where((s <= t) if k == 0 else (s >= t), scores, 0.0)
        for pair in range(heads // 2):
            lanes = slice(pair * 128, (pair + 1) * 128)
            x = u[k, at, :, lanes]
            weights = []
            for h in (2 * pair, 2 * pair + 1):
                gap = cols[k, at, :, h : h + 1] + rows[k, at, h : h + 1, :]
                weights.append((scores * jnp.exp2(jnp.minimum(gap, 64.0))).astype(BF16))
            zero = jnp.zeros_like(x)
            both = jnp.concatenate(
                [jnp.where(s < HEAD_DIM, x, zero), jnp.where(s >= HEAD_DIM, x, zero)], axis=0
            )
            y = jnp.dot(jnp.concatenate(weights, axis=1), both, preferred_element_type=F32)
            local[k, at, :, lanes] = (y + x.astype(F32) * skip[k : k + 1, lanes]).astype(BF16)

    def finish(k, at, first):
        @pl.when(first)
        def _():
            to_partner(entering, beside, 3, k).wait()
            mine_first = core == k
            for o in range(n):
                own = core == o % 2
                enter = jnp.where(
                    own, entering[k, o // 2].astype(F32), beside[k, o // 2].astype(F32)
                )
                after = enter * decay_of(other[k, o, height:]) + other[k, o, 0:height].astype(F32)
                state[share(o)] = jnp.where(mine_first, enter, after)

        cum = cols[k, at]
        end = cum[CHUNK - 1 : CHUNK] if k == 0 else cum[0:1]
        scale = expand(jnp.exp2(cum), e2_ref[...])
        carried = jnp.dot(
            u[k, at, :, inner + STATE :], state[...].astype(BF16), preferred_element_type=F32
        )
        y = local[k, at].astype(F32) + scale * carried
        half = 0.5 * gate_ref[...].astype(F32)
        g = y * (half + half * jnp.tanh(half))
        inverse = lax.rsqrt(jnp.mean(g * g, axis=-1, keepdims=True) + 1e-05)
        factor = expand(jnp.broadcast_to(jnp.exp2(end), (8, heads)), e3_ref[...])[0:1]
        state[...] = state[...] * factor + piece[k, at].astype(F32)
        return g * inverse * gain_ref[k : k + 1, :]

    @pl.when(step < chunks)
    def _():
        prepare(0, chunks - 1 - step, step == 0, step == chunks - 1)

    @pl.when((step >= chunks) & (step < 2 * chunks))
    def _():
        prepare(1, step - chunks, step == chunks, step == 2 * chunks - 1)

    for k in range(2):
        for number, stage in enumerate((per_chip, scan, back)):
            pl.when(step == (1 + k) * chunks + AT[k][number])(functools.partial(stage, k))

    @pl.when((step >= 2 * chunks) & (step < 3 * chunks))
    def _():
        at = step - 2 * chunks
        diagonal(0, at)
        diagonal(1, at)

    @pl.when((step >= 3 * chunks) & (step < 4 * chunks))
    def _():
        at = step - 3 * chunks
        kept[at] = finish(0, at, step == 3 * chunks)

    @pl.when(step >= 4 * chunks)
    def _():
        at = 5 * chunks - 1 - step
        out_ref[...] = (kept[at] + finish(1, at, step == 4 * chunks)).astype(BF16)

    @pl.when(step == 5 * chunks - 1)
    def _():
        for k in range(2):
            wait_chips(summary, send_sem, 1, k)
            wait_chips(reply, send_sem, 2, k)


def on_device(
    conv_input,
    gate_input,
    step_raw,
    filter_taps,
    filter_bias,
    step_bias,
    log_rate,
    skip_scale,
    norm_gain,
):
    length, channels = conv_input.shape
    heads = step_raw.shape[1]
    inner = heads * HEAD_DIM
    chunks = length // CHUNK
    n = lax.axis_size("seq")
    height = STATE * (inner // 128) // n
    per = CHUNK // HALO
    last = chunks * per - 1
    whole = lambda *shape: pl.BlockSpec(shape, lambda *_: (0,) * len(shape))

    def taken(i):
        return jnp.where(i < chunks, chunks - 1 - i, jnp.minimum(i - chunks, chunks - 1))

    def given(i):
        return jnp.where(i < 4 * chunks, jnp.clip(i - 3 * chunks, 0, chunks - 1), 5 * chunks - 1 - i)

    return pl.pallas_call(
        functools.partial(mixer_kernel, heads, n),
        grid=(5 * chunks,),
        in_specs=[
            pl.BlockSpec((HALO, channels), lambda i: (last, 0)),
            pl.BlockSpec((HALO, channels), lambda i: (0, 0)),
            pl.BlockSpec((HALO, channels), lambda i: (jnp.maximum(taken(i) * per - 1, 0), 0)),
            pl.BlockSpec((CHUNK, channels), lambda i: (taken(i), 0)),
            pl.BlockSpec((HALO, channels), lambda i: (jnp.minimum(taken(i) * per + per, last), 0)),
            pl.BlockSpec((heads, CHUNK), lambda i: (0, taken(i))),
            pl.BlockSpec((CHUNK, inner), lambda i: (given(i), 0)),
            whole(*filter_taps.shape),
            whole(*filter_bias.shape),
            whole(heads, 2),
            whole(heads, 2),
            whole(2, heads),
            whole(2, inner),
        ],
        out_specs=pl.BlockSpec(
            (CHUNK, inner), lambda i: (jnp.minimum(5 * chunks - 1 - i, chunks - 1), 0)
        ),
        out_shape=jax.ShapeDtypeStruct((length, inner), BF16),
        scratch_shapes=[
            pltpu.VMEM((CHUNK + 2 * HALO, channels), F32),
            pltpu.VMEM((2, chunks, CHUNK, channels), BF16),
            pltpu.VMEM((2, chunks, STATE, inner), BF16),
            pltpu.VMEM((2, chunks, CHUNK, inner), BF16),
            pltpu.VMEM((chunks, CHUNK, inner), F32),
            pltpu.VMEM((2, chunks, CHUNK, heads), F32),
            pltpu.VMEM((2, chunks, heads, CHUNK), F32),
            pltpu.VMEM((STATE, inner), F32),
            pltpu.VMEM((8, heads), F32),
            pltpu.VMEM((2, HALO, channels), BF16),
            pltpu.VMEM((2, HALO, channels), BF16),
            pltpu.VMEM((2, n, height + TILE, 128), BF16),
            pltpu.VMEM((2, n, height + TILE, 128), BF16),
            pltpu.VMEM((2, n // 2, height + TILE, 128), BF16),
            pltpu.VMEM((2, n // 2, height + TILE, 128), BF16),
            pltpu.VMEM((2, n // 2, height, 128), BF16),
            pltpu.VMEM((2, n // 2, height, 128), BF16),
            pltpu.VMEM((2, n // 2, height, 128), BF16),
            pltpu.VMEM((2 * heads, inner), BF16),
            pltpu.VMEM((3 * heads, inner), BF16),
            pltpu.VMEM((8, inner), F32),
            pltpu.SemaphoreType.DMA((2,)),
            pltpu.SemaphoreType.DMA((2,)),
            pltpu.SemaphoreType.DMA((4, 2)),
            pltpu.SemaphoreType.DMA((4, 2)),
        ],
        compiler_params=pltpu.CompilerParams(
            collective_id=0, has_side_effects=True, vmem_limit_bytes=60 * 1024 * 1024
        ),
    )(
        conv_input,
        conv_input,
        conv_input,
        conv_input,
        conv_input,
        step_raw.T,
        gate_input,
        filter_taps,
        filter_bias,
        step_bias.T,
        log_rate.T,
        skip_scale,
        norm_gain,
    )


def solution(mesh):
    return jax.shard_map(
        on_device,
        mesh=mesh,
        in_specs=(P(("groups", "seq"), None),) * 3 + (P(),) * 6,
        out_specs=P(("groups", "seq"), None),
        check_vma=False,
    )
```

```python
import functools

import jax
import jax.numpy as jnp
from jax import lax
from jax.experimental import pallas as pl
from jax.experimental.pallas import tpu as pltpu
from jax.sharding import PartitionSpec as P

HEAD_DIM = 64
STATE = 128
CHUNK = 128
HALO = 16
TILE = 16
AT = ((2, 6, 11), (2, 6, 12))
MESH = pl.DeviceIdType.MESH
LOG2E = 1.4426950408889634
F32 = jnp.float32
BF16 = jnp.bfloat16


def expander(heads, copies):
    row = lax.broadcasted_iota(jnp.int32, (heads * copies, heads * HEAD_DIM), 0) % heads
    col = lax.broadcasted_iota(jnp.int32, (heads * copies, heads * HEAD_DIM), 1) // HEAD_DIM
    return (row == col).astype(BF16)


def expand(values, matrix):
    high = values.astype(BF16)
    rest = values - high.astype(F32)
    low = rest.astype(BF16)
    parts = [high, low]
    heads = values.shape[1]
    if matrix.shape[0] == 3 * heads:
        parts.append((rest - low.astype(F32)).astype(BF16))
    return jnp.dot(jnp.concatenate(parts, axis=1), matrix, preferred_element_type=F32)


def mixer_kernel(
    heads,
    n,
    tail_ref,
    head_ref,
    prev_ref,
    cur_ref,
    next_ref,
    raw_ref,
    gate_ref,
    taps_ref,
    bias_ref,
    sbias_ref,
    lrate_ref,
    skip_ref,
    gain_ref,
    out_ref,
    buf,
    u,
    piece,
    local,
    kept,
    cols,
    rows,
    state,
    run,
    edge,
    halo,
    message,
    other,
    summary,
    got,
    reply,
    entering,
    beside,
    e2_ref,
    e3_ref,
    skip,
    edge_send,
    edge_recv,
    send_sem,
    recv_sem,
):
    step = pl.program_id(0)
    chunks = u.shape[1]
    inner = heads * HEAD_DIM
    channels = cur_ref.shape[1]
    me = lax.axis_index("seq")
    chips = n // 2
    chip = me // 2
    core = lax.rem(me, 2)
    partner = me + 1 - 2 * core
    height = STATE * (inner // 128) // n
    share = lambda o: (
        slice(o * height % STATE, o * height % STATE + height),
        slice(o * height // STATE * 128, o * height // STATE * 128 + 128),
    )

    def to_edge(side):
        return pltpu.make_async_remote_copy(
            src_ref=edge.at[side],
            dst_ref=halo.at[side],
            send_sem=edge_send.at[side],
            recv_sem=edge_recv.at[side],
            device_id={"seq": lax.rem(me + (1 if side == 0 else n - 1), n)},
            device_id_type=MESH,
        )

    def to_partner(source, target, number, k):
        return pltpu.make_async_remote_copy(
            src_ref=source.at[k],
            dst_ref=target.at[k],
            send_sem=send_sem.at[number, k],
            recv_sem=recv_sem.at[number, k],
            device_id={"seq": partner},
            device_id_type=MESH,
        )

    def to_chips(source, target, number, k):
        @pl.loop(1, chips)
        def _(p):
            peer = lax.rem(chip + p, chips)
            pltpu.make_async_remote_copy(
                src_ref=source.at[k, peer],
                dst_ref=target.at[k, chip],
                send_sem=send_sem.at[number, k],
                recv_sem=recv_sem.at[number, k],
                device_id={"seq": 2 * peer + core},
                device_id_type=MESH,
            ).start()

    def wait_chips(ref, sem, number, k):
        part = ref.at[k, pl.ds(0, chips - 1)]
        pltpu.make_async_copy(part, part, sem.at[number, k]).wait()

    @pl.when(step == 0)
    def _():
        barrier = pltpu.get_barrier_semaphore()

        def greet(peer):
            pl.semaphore_signal(barrier, inc=1, device_id={"seq": peer}, device_id_type=MESH)

        greet(lax.rem(me + 1, n))
        greet(lax.rem(me + n - 1, n))

        @pl.loop(1, chips)
        def _(p):
            greet(2 * lax.rem(chip + p, chips) + core)

        edge[0] = tail_ref[...]
        edge[1] = head_ref[...]
        e2_ref[...] = expander(heads, 2)
        e3_ref[...] = expander(heads, 3)
        scales = jnp.concatenate([skip_ref[...]] * 4, axis=0)
        skip[...] = expand(scales, e3_ref[...])
        pl.semaphore_wait(barrier, chips + 1)
        to_edge(0).start()
        to_edge(1).start()

    t = lax.broadcasted_iota(jnp.int32, (CHUNK, CHUNK), 0)
    s = lax.broadcasted_iota(jnp.int32, (CHUNK, CHUNK), 1)

    def prepare(k, at, first, last):
        @pl.when(first)
        def _():
            state[...] = jnp.zeros_like(state)
            run[...] = jnp.zeros_like(run)

        buf[0:HALO] = prev_ref[...].astype(F32)
        buf[HALO : HALO + CHUNK] = cur_ref[...].astype(F32)
        buf[HALO + CHUNK :] = next_ref[...].astype(F32)

        @pl.when(last)
        def _():
            to_edge(k).wait()
            if k == 0:
                buf[0:HALO] = jnp.where(me == 0, 0.0, halo[0].astype(F32))
            else:
                buf[HALO + CHUNK :] = jnp.where(me == n - 1, 0.0, halo[1].astype(F32))

        width = 256
        for c in range(channels // width):
            lanes = slice(c * width, (c + 1) * width)
            half = None
            for j in range(4):
                start = HALO + (j - 3 if k == 0 else 3 - j)
                term = buf[start : start + CHUNK, lanes] * (0.5 * taps_ref[k, j : j + 1, lanes])
                half = 0.5 * bias_ref[k : k + 1, lanes] + term if half is None else half + term
            u[k, at, :, lanes] = (half + half * jnp.tanh(half)).astype(BF16)

        dt = jax.nn.softplus(raw_ref[...].astype(F32) + sbias_ref[:, k : k + 1])
        a = dt * (-LOG2E * jnp.exp(lrate_ref[:, k : k + 1]))
        tri = ((t <= s) if k == 0 else (t >= s)).astype(F32)
        across = jnp.dot(a, tri, precision=lax.Precision.HIGHEST, preferred_element_type=F32)
        rows[k, at] = jnp.log2(dt) - across
        cum = across.T
        ahead = rows[k, at].T
        end = cum[CHUNK - 1 : CHUNK] if k == 0 else cum[0:1]
        cols[k, at] = cum
        weight = expand(jnp.exp2(end + ahead), e2_ref[...])
        xs = (u[k, at, :, :inner].astype(F32) * weight).astype(BF16)
        bt = u[k, at, :, inner : inner + STATE].T
        part = jnp.dot(bt, xs, preferred_element_type=F32)
        piece[k, at] = part.astype(BF16)
        before = run[0:1, :]
        factor = expand(jnp.broadcast_to(jnp.exp2(before), (8, heads)), e3_ref[...])[0:1]
        state[...] = state[...] + part * factor
        run[0:1, :] = before + end

        @pl.when(last)
        def _():
            decay = expand(jnp.exp2(jnp.broadcast_to(run[0:1, :], (TILE, heads))), e3_ref[...])
            high = decay.astype(BF16).astype(F32)
            which = lax.broadcasted_iota(jnp.int32, (TILE, inner), 0)
            tile = jnp.where(which == 0, high, jnp.where(which == 1, decay - high, 0.0))
            for o in range(n):
                where = share(o)
                message[k, o, 0:height] = state[where].astype(BF16)
                message[k, o, height:] = tile[:, where[1]].astype(BF16)
            to_partner(message, other, 0, k).start()

    def decay_of(tile):
        return tile[0:1].astype(F32) + tile[1:2].astype(F32)

    def per_chip(k):
        to_partner(message, other, 0, k).wait()
        mine_first = core == k
        which = lax.broadcasted_iota(jnp.int32, (TILE, 128), 0)

        @pl.loop(0, chips)
        def _(q):
            o = 2 * q + core
            mine = message[k, o, 0:height].astype(F32)
            theirs = other[k, o, 0:height].astype(F32)
            my_decay = decay_of(message[k, o, height:])
            their_decay = decay_of(other[k, o, height:])
            total = jnp.where(mine_first, mine * their_decay + theirs, theirs * my_decay + mine)
            decay = my_decay * their_decay
            high = decay.astype(BF16).astype(F32)
            tile = jnp.where(which == 0, high, jnp.where(which == 1, decay - high, 0.0))
            summary[k, q, 0:height] = total.astype(BF16)
            summary[k, q, height:] = tile.astype(BF16)

        got[k, chip] = summary[k, chip]
        to_chips(summary, got, 1, k)

    def scan(k):
        wait_chips(got, recv_sem, 1, k)

        def one(j, held):
            j = j if k == 0 else chips - 1 - j
            reply[k, j] = held.astype(BF16)
            decay = decay_of(got[k, j, height:])
            return held * decay + got[k, j, 0:height].astype(F32)

        lax.fori_loop(0, chips, one, jnp.zeros((height, 128), F32))
        entering[k, chip] = reply[k, chip]
        to_chips(reply, entering, 2, k)

    def back(k):
        wait_chips(entering, recv_sem, 2, k)
        to_partner(entering, beside, 3, k).start()

    def diagonal(k, at):
        b = u[k, at, :, inner : inner + STATE]
        c = u[k, at, :, inner + STATE :]
        scores = lax.dot_general(c, b, (((1,), (1,)), ((), ())), preferred_element_type=F32)
        scores = jnp.where((s <= t) if k == 0 else (s >= t), scores, 0.0)
        for pair in range(heads // 2):
            lanes = slice(pair * 128, (pair + 1) * 128)
            x = u[k, at, :, lanes]
            weights = []
            for h in (2 * pair, 2 * pair + 1):
                gap = cols[k, at, :, h : h + 1] + rows[k, at, h : h + 1, :]
                weights.append((scores * jnp.exp2(jnp.minimum(gap, 64.0))).astype(BF16))
            zero = jnp.zeros_like(x)
            both = jnp.concatenate(
                [jnp.where(s < HEAD_DIM, x, zero), jnp.where(s >= HEAD_DIM, x, zero)], axis=0
            )
            y = jnp.dot(jnp.concatenate(weights, axis=1), both, preferred_element_type=F32)
            local[k, at, :, lanes] = (y + x.astype(F32) * skip[k : k + 1, lanes]).astype(BF16)

    def finish(k, at, first):
        @pl.when(first)
        def _():
            to_partner(entering, beside, 3, k).wait()
            mine_first = core == k
            for o in range(n):
                own = core == o % 2
                enter = jnp.where(
                    own, entering[k, o // 2].astype(F32), beside[k, o // 2].astype(F32)
                )
                after = enter * decay_of(other[k, o, height:]) + other[k, o, 0:height].astype(F32)
                state[share(o)] = jnp.where(mine_first, enter, after)

        cum = cols[k, at]
        end = cum[CHUNK - 1 : CHUNK] if k == 0 else cum[0:1]
        scale = expand(jnp.exp2(cum), e2_ref[...])
        carried = jnp.dot(
            u[k, at, :, inner + STATE :], state[...].astype(BF16), preferred_element_type=F32
        )
        y = local[k, at].astype(F32) + scale * carried
        half = 0.5 * gate_ref[...].astype(F32)
        g = y * (half + half * jnp.tanh(half))
        inverse = lax.rsqrt(jnp.mean(g * g, axis=-1, keepdims=True) + 1e-05)
        factor = expand(jnp.broadcast_to(jnp.exp2(end), (8, heads)), e3_ref[...])[0:1]
        state[...] = state[...] * factor + piece[k, at].astype(F32)
        return g * inverse * gain_ref[k : k + 1, :]

    @pl.when(step < chunks)
    def _():
        prepare(0, chunks - 1 - step, step == 0, step == chunks - 1)

    @pl.when((step >= chunks) & (step < 2 * chunks))
    def _():
        prepare(1, step - chunks, step == chunks, step == 2 * chunks - 1)

    for k in range(2):
        for number, stage in enumerate((per_chip, scan, back)):
            pl.when(step == (1 + k) * chunks + AT[k][number])(functools.partial(stage, k))

    @pl.when((step >= 2 * chunks) & (step < 3 * chunks))
    def _():
        at = step - 2 * chunks
        diagonal(0, at)
        diagonal(1, at)

    @pl.when((step >= 3 * chunks) & (step < 4 * chunks))
    def _():
        at = step - 3 * chunks
        kept[at] = finish(0, at, step == 3 * chunks)

    @pl.when(step >= 4 * chunks)
    def _():
        at = 5 * chunks - 1 - step
        out_ref[...] = (kept[at] + finish(1, at, step == 4 * chunks)).astype(BF16)

    @pl.when(step == 5 * chunks - 1)
    def _():
        for k in range(2):
            wait_chips(summary, send_sem, 1, k)
            wait_chips(reply, send_sem, 2, k)


def on_device(
    conv_input,
    gate_input,
    step_raw,
    filter_taps,
    filter_bias,
    step_bias,
    log_rate,
    skip_scale,
    norm_gain,
):
    length, channels = conv_input.shape
    heads = step_raw.shape[1]
    inner = heads * HEAD_DIM
    chunks = length // CHUNK
    n = lax.axis_size("seq")
    height = STATE * (inner // 128) // n
    per = CHUNK // HALO
    last = chunks * per - 1
    whole = lambda *shape: pl.BlockSpec(shape, lambda *_: (0,) * len(shape))

    def taken(i):
        return jnp.where(i < chunks, chunks - 1 - i, jnp.minimum(i - chunks, chunks - 1))

    def given(i):
        return jnp.where(i < 4 * chunks, jnp.clip(i - 3 * chunks, 0, chunks - 1), 5 * chunks - 1 - i)

    return pl.pallas_call(
        functools.partial(mixer_kernel, heads, n),
        grid=(5 * chunks,),
        in_specs=[
            pl.BlockSpec((HALO, channels), lambda i: (last, 0)),
            pl.BlockSpec((HALO, channels), lambda i: (0, 0)),
            pl.BlockSpec((HALO, channels), lambda i: (jnp.maximum(taken(i) * per - 1, 0), 0)),
            pl.BlockSpec((CHUNK, channels), lambda i: (taken(i), 0)),
            pl.BlockSpec((HALO, channels), lambda i: (jnp.minimum(taken(i) * per + per, last), 0)),
            pl.BlockSpec((heads, CHUNK), lambda i: (0, taken(i))),
            pl.BlockSpec((CHUNK, inner), lambda i: (given(i), 0)),
            whole(*filter_taps.shape),
            whole(*filter_bias.shape),
            whole(heads, 2),
            whole(heads, 2),
            whole(2, heads),
            whole(2, inner),
        ],
        out_specs=pl.BlockSpec(
            (CHUNK, inner), lambda i: (jnp.minimum(5 * chunks - 1 - i, chunks - 1), 0)
        ),
        out_shape=jax.ShapeDtypeStruct((length, inner), BF16),
        scratch_shapes=[
            pltpu.VMEM((CHUNK + 2 * HALO, channels), F32),
            pltpu.VMEM((2, chunks, CHUNK, channels), BF16),
            pltpu.VMEM((2, chunks, STATE, inner), BF16),
            pltpu.VMEM((2, chunks, CHUNK, inner), BF16),
            pltpu.VMEM((chunks, CHUNK, inner), F32),
            pltpu.VMEM((2, chunks, CHUNK, heads), F32),
            pltpu.VMEM((2, chunks, heads, CHUNK), F32),
            pltpu.VMEM((STATE, inner), F32),
            pltpu.VMEM((8, heads), F32),
            pltpu.VMEM((2, HALO, channels), BF16),
            pltpu.VMEM((2, HALO, channels), BF16),
            pltpu.VMEM((2, n, height + TILE, 128), BF16),
            pltpu.VMEM((2, n, height + TILE, 128), BF16),
            pltpu.VMEM((2, n // 2, height + TILE, 128), BF16),
            pltpu.VMEM((2, n // 2, height + TILE, 128), BF16),
            pltpu.VMEM((2, n // 2, height, 128), BF16),
            pltpu.VMEM((2, n // 2, height, 128), BF16),
            pltpu.VMEM((2, n // 2, height, 128), BF16),
            pltpu.VMEM((2 * heads, inner), BF16),
            pltpu.VMEM((3 * heads, inner), BF16),
            pltpu.VMEM((8, inner), F32),
            pltpu.SemaphoreType.DMA((2,)),
            pltpu.SemaphoreType.DMA((2,)),
            pltpu.SemaphoreType.DMA((4, 2)),
            pltpu.SemaphoreType.DMA((4, 2)),
        ],
        compiler_params=pltpu.CompilerParams(
            collective_id=0, has_side_effects=True, vmem_limit_bytes=60 * 1024 * 1024
        ),
    )(
        conv_input,
        conv_input,
        conv_input,
        conv_input,
        conv_input,
        step_raw.T,
        gate_input,
        filter_taps,
        filter_bias,
        step_bias.T,
        log_rate.T,
        skip_scale,
        norm_gain,
    )


def solution(mesh):
    return jax.shard_map(
        on_device,
        mesh=mesh,
        in_specs=(P(("groups", "seq"), None),) * 3 + (P(),) * 6,
        out_specs=P(("groups", "seq"), None),
        check_vma=False,
    )
```
